256 devices in a mesh: tri: 256 (over y, x, z, core).
Axes of the slice: x: 4, y: 4, z: 8, core: 2. Of those that a mesh axis runs over, the one named last changes fastest.
Arguments:
- matrix_tiles: bfloat16 [4096, 12, 128, 128], P('tri'), may hold values from -0.109375 to 0.109375
- columns: int32 [4096, 12], P('tri'), may hold values from 0 to 4095, as said below
- vectors: bfloat16 [16, 524288], P(None, 'tri'), may hold values from -6 to 6
- center: float32 [1], replicated, may hold values from -1 to 1
- halfwidth: float32 [1], replicated, may hold values from 1.5 to 3
Outputs:
- filtered_one: float32 [16, 524288], P(None, 'tri')
- filtered_two: float32 [16, 524288], P(None, 'tri')
The draws below stay inside these ranges and needn't reach their ends.
Inputs may be any that keep to these rules, and one draw needn't show every extreme that they name: For block row i, columns[i, k] lies between max(0, (i // 16 - 4) * 16) and i; columns[i, 0] = i and columns[i, 1] = max(0, (i // 16 - 4) * 16); entries may repeat, and repeated tiles add.
All inputs are finite; a program needn't handle non-finite values.
Results may differ from the reference program's by a relative error of at most 0.0018.
Values may be sent and summed in bfloat16 or wider, within the bound.
A program may use at most 64 MiB of HBM per device.

```python
import jax
import jax.numpy as jnp
from jax import lax

BS = 128
RB = 16
KT = 12
VEC = 16
SPAN = 4
NB = 4096
N = 524288


def draw_columns(key, part):
    key = jax.random.fold_in(key, 7)
    row_ids = jnp.arange(NB, dtype=jnp.int32)
    lowest = jnp.maximum(0, (row_ids // RB - SPAN) * RB).astype(jnp.int32)
    picked = jax.random.randint(key, (NB, KT), lowest[:, None], row_ids[:, None] + 1, dtype=jnp.int32)
    picked = picked.at[:, 0].set(row_ids)
    return picked.at[:, 1].set(lowest)


def level_of(rng, shape, split, least, largest):
    def one(dim, blocks):
        steps = jax.random.uniform(jax.random.fold_in(jax.random.fold_in(rng, 6), dim), (blocks,), jnp.float32, least / len(split), largest / len(split))
        return jnp.repeat(jnp.exp(steps), shape[dim] // blocks).reshape((-1,) + (1,) * (len(shape) - dim - 1))

    factor_of = one(*split[0])
    for cut in split[1:]:
        factor_of = factor_of * one(*cut)
    return factor_of


def scatter_about(key, extent, scale, limit, cuts=(), kind=jnp.bfloat16):
    result = scale * jax.random.normal(key, extent, jnp.float32)
    if cuts:
        result = result * level_of(key, extent, cuts, -0.22, 0.18)
    return jnp.clip(result, -limit, limit).astype(kind)


def setup_inputs(seed: int = 0) -> dict:
    keys = jax.random.split(jax.random.key(seed), 6)
    matrix_tiles = scatter_about(keys[0], (NB, KT, BS, BS), (2 * KT * BS) ** -0.5, 0.109375, ((0, 256),))
    columns = draw_columns(jax.random.fold_in(keys[5], 71), 0)
    vectors = scatter_about(keys[2], (VEC, N), 1.0, 6.0, ((1, 256),))
    center = jnp.clip(jax.random.uniform(keys[3], (1,), jnp.float32, -1.0, 1.0), -1.0, 1.0)
    halfwidth = jnp.clip(jax.random.uniform(keys[4], (1,), jnp.float32, 1.5, 3.0), 1.5, 3.0)
    return {"matrix_tiles": matrix_tiles, "columns": columns, "vectors": vectors, "center": center, "halfwidth": halfwidth}


def apply_hamiltonian(matrix_tiles, columns, blocks):
    count_blocks = blocks.shape[0]
    row_ids = jnp.arange(count_blocks, dtype=jnp.int32)
    weight = jnp.where(columns == row_ids[:, None], 0.5, 1.0).astype(jnp.float32)
    groups = count_blocks // RB
    tile_groups = matrix_tiles.reshape(groups, RB, KT, BS, BS)
    column_groups = columns.reshape(groups, RB, KT)
    weight_groups = weight.reshape(groups, RB, KT)
    block_groups = blocks.reshape(groups, RB, VEC, BS)

    def step_group(buffer, items):
        tile_part, column_part, weight_part, own_part = items
        picked = jnp.take(blocks, column_part.reshape(-1), axis=0).reshape(RB, KT, VEC, BS)
        forward = jnp.einsum("rkvc,rkac->rkva", picked.astype(jnp.float32), tile_part.astype(jnp.float32))
        forward = jnp.sum(forward * weight_part[:, :, None, None], axis=1)
        behind = jnp.einsum("rva,rkac->rkvc", own_part.astype(jnp.float32), tile_part.astype(jnp.float32))
        behind = behind * weight_part[:, :, None, None]
        buffer = buffer.at[column_part.reshape(-1)].add(behind.reshape(RB * KT, VEC, BS))
        return buffer, forward

    start = jnp.zeros((count_blocks, VEC, BS), jnp.float32)
    buffer, forward_all = lax.scan(step_group, start, (tile_groups, column_groups, weight_groups, block_groups))
    return forward_all.reshape(count_blocks, VEC, BS) + buffer


def reference(matrix_tiles, columns, vectors, center, halfwidth):
    count_blocks = matrix_tiles.shape[0]
    blocks = vectors.reshape(VEC, count_blocks, BS).transpose(1, 0, 2)
    initial = blocks.astype(jnp.float32)
    product_one = apply_hamiltonian(matrix_tiles, columns, blocks)
    first = (product_one - center[0] * initial) / halfwidth[0]
    rounded = first.astype(jnp.bfloat16)
    product_two = apply_hamiltonian(matrix_tiles, columns, rounded)
    second = 2.0 * (product_two - center[0] * first) / halfwidth[0] - initial
    first_out = first.transpose(1, 0, 2).reshape(VEC, count_blocks * BS)
    second_out = second.transpose(1, 0, 2).reshape(VEC, count_blocks * BS)
    return first_out, second_out
```

```python
import functools

import jax
import jax.numpy as jnp
from jax import lax
from jax.experimental import pallas as pl
from jax.experimental.pallas import tpu as pltpu
from jax.sharding import PartitionSpec as P

SPAN = 4
CHAINS = 2
TOP = 32766.0
MESH = pl.DeviceIdType.MESH
F32 = jnp.float32
LAST_ROW = 16
SLOT_ROW = LAST_ROW + 8 * CHAINS
ON_LAST = (((1,), (1,)), ((), ()))


def kernel(
    n,
    tiles_hbm,
    cols_v,
    cols_s,
    vec_v,
    center_s,
    half_s,
    out1,
    out2,
    tiles,
    win0,
    win1,
    sums,
    ahead,
    total,
    coded,
    landed,
    tab_v,
    tab_s,
    tile_sem,
    tab_sem,
    xsend,
    xrecv,
    psend,
    precv,
):
    rows, kt, width, _ = tiles.shape
    nv = vec_v.shape[0]
    half = rows // CHAINS
    none = half * kt
    me = lax.axis_index("tri")
    lowest = (me - SPAN) * rows

    def load(r):
        return pltpu.make_async_copy(tiles_hbm.at[r], tiles.at[r], tile_sem.at[r])

    for j in range(half):
        for c in range(CHAINS):
            load(c * half + j).start()

    barrier = pltpu.get_barrier_semaphore()
    for o in range(1, SPAN + 1):
        for d in (o, n - o):
            pl.semaphore_signal(
                barrier, inc=1, device_id=(lax.rem(me + d, n),), device_id_type=MESH
            )

    own = SPAN * rows
    win = (win0, win1)
    for r in range(rows):
        win0[own + r] = vec_v[:, r * width : (r + 1) * width]

    sums[:, none] = jnp.zeros((CHAINS, nv, width), F32)
    tid = lax.broadcasted_iota(jnp.int32, (half, kt), 0) * kt + lax.broadcasted_iota(
        jnp.int32, (half, kt), 1
    )
    lane = lax.broadcasted_iota(jnp.int32, (8, 128), 1)
    slots = jnp.clip(cols_v[...] - lowest, 0, (SPAN + 1) * rows - 1)
    tab_v[SLOT_ROW : SLOT_ROW + rows, 0:kt] = slots
    for c in range(CHAINS):
        mine = slots[c * half : (c + 1) * half]

        def note(j, carry):
            prev, last = carry
            for k in range(kt):
                s = cols_s[c * half + j, k] - lowest
                t = j * kt + k
                prev = jnp.where((mine == s) & (tid > t), t, prev)
                last = jnp.where(lane == s, t, last)
            return prev, last

        prev, last = lax.fori_loop(
            0,
            half,
            note,
            (jnp.full((half, kt), none, jnp.int32), jnp.full((8, 128), none, jnp.int32)),
        )
        tab_v[c * half : (c + 1) * half, 0:kt] = prev
        tab_v[LAST_ROW + 8 * c : LAST_ROW + 8 * (c + 1), :] = last
    tab_copy = pltpu.make_async_copy(tab_v, tab_s, tab_sem)
    tab_copy.start()

    pl.semaphore_wait(barrier, 2 * SPAN)

    def vector_copy(step, o):
        return pltpu.make_async_remote_copy(
            src_ref=win[step].at[pl.ds(own, rows)],
            dst_ref=win[step].at[pl.ds((SPAN - o) * rows, rows)],
            send_sem=xsend.at[step, o - 1],
            recv_sem=xrecv.at[step, o - 1],
            device_id=(lax.rem(me + o, n),),
            device_id_type=MESH,
        )

    def product_copy(step, g):
        return pltpu.make_async_remote_copy(
            src_ref=coded.at[step, g],
            dst_ref=landed.at[step, g],
            send_sem=psend.at[step, g],
            recv_sem=precv.at[step, g],
            device_id=(lax.rem(me + n - SPAN + g, n),),
            device_id_type=MESH,
        )

    def transposed_products(step):
        def body(j, carry):
            for c in range(CHAINS):
                r = c * half + j
                if step == 0:
                    load(r).wait()
                x = win[step][own + r]
                for k in range(0, kt, 2):
                    pair = jnp.concatenate([tiles[r, k], tiles[r, k + 1]], axis=1)
                    both = jnp.dot(x, pair, preferred_element_type=F32)
                    for i in range(2):
                        s = tab_s[SLOT_ROW + r, k + i]
                        weight = jnp.where(s == own + r, 0.5, 1.0).astype(F32)
                        part = both[:, i * width : (i + 1) * width] * weight
                        before = tab_s[r, k + i]
                        sums[c, j * kt + k + i] = part + sums[c, before]
            return carry

        lax.fori_loop(0, half, body, 0)

    def slot_sum(s):
        return sum(sums[c, tab_s[LAST_ROW + 8 * c, s]] for c in range(CHAINS))

    def send_products(step):
        def body(g, carry):
            most = jnp.zeros((nv, width), F32)
            for r in range(rows):
                v = slot_sum(g * rows + r)
                total[r] = v
                most = jnp.maximum(most, jnp.abs(v))
            peak = jnp.maximum(jnp.max(most, axis=1, keepdims=True), 1e-30)
            power = jnp.broadcast_to(jnp.ceil(jnp.log2(peak)), (nv, width))
            scale = jnp.exp2(-power) * TOP
            for r in range(rows):
                coded[step, g, r] = (
                    jnp.round(total[r] * scale).astype(jnp.int32).astype(jnp.int16)
                )
            coded[step, g, rows] = power.astype(jnp.int32).astype(jnp.int16)
            product_copy(step, g).start()
            return carry

        lax.fori_loop(0, SPAN, body, 0)

    def forward(step):
        def body(r, carry):
            picked = []
            for k in range(kt):
                s = tab_s[SLOT_ROW + r, k]
                weight = jnp.where(s == own + r, 0.5, 1.0).astype(F32)
                picked.append(win[step][s] * jnp.full((nv, width), weight).astype(jnp.bfloat16))
            x = jnp.concatenate(picked, axis=1)
            w = jnp.concatenate([tiles[r, k] for k in range(kt)], axis=1)
            ahead[r] = lax.dot_general(x, w, ON_LAST, preferred_element_type=F32)
            return carry

        lax.fori_loop(0, rows, body, 0)

    center = center_s[0]
    inv = 1.0 / jnp.full((nv, width), half_s[0], F32)

    for step in range(2):
        for o in range(1, SPAN + 1):
            vector_copy(step, o).start()
        if step == 0:
            tab_copy.wait()
        transposed_products(step)
        send_products(step)
        for o in range(1, SPAN + 1):
            vector_copy(step, o).wait_recv()
        forward(step)
        scales = []
        for g in range(SPAN):
            product_copy(step, g).wait_recv()
        for g in range(SPAN):
            power = landed[step, g, rows].astype(jnp.int32).astype(F32)
            scales.append(jnp.exp2(power) * (1.0 / TOP))
        for r in range(rows):
            cut = slice(r * width, (r + 1) * width)
            v = ahead[r] + slot_sum(own + r)
            for g in range(SPAN):
                v = v + landed[step, g, r].astype(jnp.int32).astype(F32) * scales[g]
            x0 = win0[own + r].astype(F32)
            if step == 0:
                first = (v - center * x0) * inv
                out1[:, cut] = first
                win1[own + r] = first.astype(jnp.bfloat16)
            else:
                out2[:, cut] = 2.0 * (v - center * out1[:, cut]) * inv - x0

    for step in range(2):
        for o in range(1, SPAN + 1):
            vector_copy(step, o).wait_send()
        for g in range(SPAN):
            product_copy(step, g).wait_send()


def per_device(n, matrix_tiles, columns, vectors, center, halfwidth):
    rows, kt, width, _ = matrix_tiles.shape
    nv = vectors.shape[0]
    vmem = pl.BlockSpec(memory_space=pltpu.VMEM)
    smem = pl.BlockSpec(memory_space=pltpu.SMEM)
    out = jax.ShapeDtypeStruct(vectors.shape, F32)
    chain = rows // CHAINS * kt
    return pl.pallas_call(
        functools.partial(kernel, n),
        out_shape=(out, out),
        in_specs=[pl.BlockSpec(memory_space=pl.ANY), vmem, smem, vmem, smem, smem],
        out_specs=(vmem, vmem),
        scratch_shapes=[
            pltpu.VMEM(matrix_tiles.shape, jnp.bfloat16),
            pltpu.VMEM(((SPAN + 1) * rows, nv, width), jnp.bfloat16),
            pltpu.VMEM(((SPAN + 1) * rows, nv, width), jnp.bfloat16),
            pltpu.VMEM((CHAINS, chain + 1, nv, width), F32),
            pltpu.VMEM((rows, nv, width), F32),
            pltpu.VMEM((rows, nv, width), F32),
            pltpu.VMEM((2, SPAN, rows + 1, nv, width), jnp.int16),
            pltpu.VMEM((2, SPAN, rows + 1, nv, width), jnp.int16),
            pltpu.VMEM((SLOT_ROW + rows, 128), jnp.int32),
            pltpu.SMEM((SLOT_ROW + rows, 128), jnp.int32),
            pltpu.SemaphoreType.DMA((rows,)),
            pltpu.SemaphoreType.DMA,
            pltpu.SemaphoreType.DMA((2, SPAN)),
            pltpu.SemaphoreType.DMA((2, SPAN)),
            pltpu.SemaphoreType.DMA((2, SPAN)),
            pltpu.SemaphoreType.DMA((2, SPAN)),
        ],
        compiler_params=pltpu.CompilerParams(
            collective_id=0, has_side_effects=True, vmem_limit_bytes=32 << 20
        ),
    )(matrix_tiles, columns, columns, vectors, center, halfwidth)


def solution(mesh):
    placed = (P("tri", None, None, None), P("tri", None), P(None, "tri"), P(), P())
    return jax.shard_map(
        functools.partial(per_device, mesh.shape["tri"]),
        mesh=mesh,
        in_specs=placed,
        out_specs=(P(None, "tri"), P(None, "tri")),
        check_vma=False,
    )
```

```python
import functools

import jax
import jax.numpy as jnp
from jax import lax
from jax.experimental import pallas as pl
from jax.experimental.pallas import tpu as pltpu
from jax.sharding import PartitionSpec as P

SPAN = 4
BEHIND_PARTS = 2
FORWARD_PARTS = 2
CHAINS = 2
TOP = 32766.0
MESH = pl.DeviceIdType.MESH
F32 = jnp.float32
LAST_ROW = 16
SLOT_ROW = LAST_ROW + 8 * CHAINS
ON_LAST = (((1,), (1,)), ((), ()))


def kernel(
    n,
    tiles_hbm,
    cols_hbm,
    vec_hbm,
    center_hbm,
    half_hbm,
    out1,
    out2,
    cols_v,
    cols_s,
    vec_v,
    center_s,
    half_s,
    tiles,
    win0,
    win1,
    sums,
    ahead,
    total,
    staged,
    shared,
    coded,
    landed,
    tab_v,
    tab_s,
    tile_sem,
    small_sem,
    tab_sem,
    xsend,
    xrecv,
    ssend,
    srecv,
    psend,
    precv,
):
    rows, kt, width, _ = tiles.shape
    nv = vec_v.shape[0]
    half = rows // CHAINS
    none = half * kt
    me = lax.axis_index("tri")
    core = lax.rem(me, 2)
    other = me + 1 - 2 * core
    lowest = (me - SPAN) * rows

    def exists(d):
        return (me + d >= 0) & (me + d < n)


    def load(r):
        return pltpu.make_async_copy(tiles_hbm.at[r], tiles.at[r], tile_sem.at[r])

    def small(i, src, dst):
        return pltpu.make_async_copy(src, dst, small_sem.at[i])

    smalls = [
        small(0, cols_hbm, cols_s),
        small(1, cols_hbm, cols_v),
        small(2, vec_hbm, vec_v),
        small(3, center_hbm, center_s),
        small(4, half_hbm, half_s),
    ]
    for copy in smalls:
        copy.start()
    for j in range(half):
        for c in range(CHAINS):
            load(c * half + j).start()

    barrier = pltpu.get_barrier_semaphore()
    pl.semaphore_signal(barrier, inc=1, device_id=(other,), device_id_type=MESH)
    for d in (2, -2, 4, -4):

        @pl.when(exists(d))
        def _():
            pl.semaphore_signal(barrier, inc=1, device_id=(me + d,), device_id_type=MESH)

    own = SPAN * rows
    win = (win0, win1)
    smalls[2].wait()
    for r in range(rows):
        win0[own + r] = vec_v[:, r * width : (r + 1) * width]
    for i, d in enumerate((4, 2)):

        @pl.when(jnp.logical_not(exists(d)))
        def _():
            for step in range(2):
                landed[step, i] = jnp.zeros(landed.shape[2:], landed.dtype)

    for step in range(2):
        shared[step, 2 * core] = jnp.zeros(shared.shape[2:], F32)

    greeted = 1 + jnp.minimum(me // 2, 2) + jnp.minimum((n - 1 - me) // 2, 2)
    pl.semaphore_wait(barrier, greeted)

    def vector_copy(step, i, src, dst, to):
        return pltpu.make_async_remote_copy(
            src_ref=win[step].at[pl.ds(src * rows, rows)],
            dst_ref=win[step].at[pl.ds(dst * rows, rows)],
            send_sem=xsend.at[step, i],
            recv_sem=xrecv.at[step, dst],
            device_id=(to,),
            device_id_type=MESH,
        )

    def vector_sends(step):
        return [
            (core == 0, vector_copy(step, 0, SPAN, SPAN - 1, other)),
            (exists(4), vector_copy(step, 1, SPAN, SPAN - 4, me + 4)),
            (exists(2), vector_copy(step, 2, SPAN, SPAN - 2, me + 2)),
        ]

    def vector_hands(step):
        return [
            (2, vector_copy(step, 3, 2, 1 + 2 * core, other), exists(-2)),
            (0, vector_copy(step, 4, 0, 1, other), exists(-4) & (core == 1)),
        ]

    def await_vectors(step, g):
        @pl.when(exists(g - SPAN))
        def _():
            vector_copy(step, 0, SPAN, g, other).wait_recv()

    def send_vectors(step):
        for wanted, copy in vector_sends(step):
            pl.when(wanted)(copy.start)

    send_vectors(0)

    for c in range(CHAINS):
        sums[c][none] = jnp.zeros((nv, width), F32)
    for copy in smalls[:2]:
        copy.wait()
    tid = lax.broadcasted_iota(jnp.int32, (half, kt), 0) * kt + lax.broadcasted_iota(
        jnp.int32, (half, kt), 1
    )
    lane = lax.broadcasted_iota(jnp.int32, (8, 128), 1)
    slots = jnp.clip(cols_v[...] - lowest, 0, (SPAN + 1) * rows - 1)
    tab_v[SLOT_ROW : SLOT_ROW + rows, 0:kt] = slots
    for c in range(CHAINS):
        mine = slots[c * half : (c + 1) * half]

        def note(j, carry):
            prev, last = carry
            for k in range(kt):
                s = cols_s[c * half + j, k] - lowest
                t = j * kt + k
                prev = jnp.where((mine == s) & (tid > t), t, prev)
                last = jnp.where(lane == s, t, last)
            return prev, last

        prev, last = lax.fori_loop(
            0,
            half,
            note,
            (jnp.full((half, kt), none, jnp.int32), jnp.full((8, 128), none, jnp.int32)),
        )
        tab_v[c * half : (c + 1) * half, 0:kt] = prev
        tab_v[LAST_ROW + 8 * c : LAST_ROW + 8 * (c + 1), :] = last
    tab_copy = pltpu.make_async_copy(tab_v, tab_s, tab_sem)
    tab_copy.start()

    def share_copy(step, i):
        return pltpu.make_async_remote_copy(
            src_ref=staged.at[step, i],
            dst_ref=shared.at[step, core + i],
            send_sem=ssend.at[step, i],
            recv_sem=srecv.at[step, core + i],
            device_id=(other,),
            device_id_type=MESH,
        )

    def await_share(step, i):
        pltpu.make_async_remote_copy(
            src_ref=staged.at[step, 0],
            dst_ref=shared.at[step, i],
            send_sem=ssend.at[step, 0],
            recv_sem=srecv.at[step, i],
            device_id=(other,),
            device_id_type=MESH,
        ).wait_recv()

    def product_copy(step, i):
        return pltpu.make_async_remote_copy(
            src_ref=coded.at[step, i],
            dst_ref=landed.at[step, i],
            send_sem=psend.at[step, i],
            recv_sem=precv.at[step, i],
            device_id=(me - SPAN + 2 * i,),
            device_id_type=MESH,
        )

    def transposed_products(step):
        def body(part, carry):
            for i in range(half // BEHIND_PARTS):
                j = part * (half // BEHIND_PARTS) + i
                if step == 0:
                    for c in range(CHAINS):
                        load(c * half + j).wait()
                for k in range(0, kt, 2):
                    for c in range(CHAINS):
                        add_pair(step, c, j, k)
            return carry

        lax.fori_loop(0, BEHIND_PARTS, body, 0)

    def add_pair(step, c, j, k):
        r = c * half + j
        pair = jnp.concatenate([tiles[r, k], tiles[r, k + 1]], axis=1)
        both = jnp.dot(win[step][own + r], pair, preferred_element_type=F32)
        for i in range(2):
            slot = tab_s[SLOT_ROW + r, k + i]
            weight = jnp.where(slot == own + r, 0.5, 1.0).astype(F32)
            part = both[:, i * width : (i + 1) * width] * weight
            before = tab_s[r, k + i]
            sums[c][j * kt + k + i] = part + sums[c][before]

    def slot_sum(s):
        return sum(sums[c][tab_s[LAST_ROW + 8 * c, s]] for c in range(CHAINS))

    def send_products(step):
        for i in range(2):
            for r in range(rows):
                staged[step, i, r] = slot_sum((2 * i + 1) * rows + r)
            share_copy(step, i).start()
        for i in range(2):
            if i == 0:
                pl.when(core == 1)(lambda: await_share(step, 0))
            else:
                await_share(step, 1)
            most = jnp.zeros((nv, width), F32)
            for r in range(rows):
                v = slot_sum(2 * i * rows + r) + shared[step, i, r]
                total[r] = v
                most = jnp.maximum(most, jnp.abs(v))
            peak = jnp.maximum(jnp.max(most, axis=1, keepdims=True), 1e-30)
            power = jnp.broadcast_to(jnp.ceil(jnp.log2(peak)), (nv, width))
            scale = jnp.exp2(-power) * TOP
            for r in range(rows):
                coded[step, i, r] = (
                    jnp.round(total[r] * scale).astype(jnp.int32).astype(jnp.int16)
                )
            coded[step, i, rows] = power.astype(jnp.int32).astype(jnp.int16)
            pl.when(exists(2 * i - SPAN))(product_copy(step, i).start)

    def forward(step):
        def body(part, carry):
            for i in range(rows // FORWARD_PARTS):
                r = part * (rows // FORWARD_PARTS) + i
                picked = []
                for k in range(kt):
                    s = tab_s[SLOT_ROW + r, k]
                    weight = jnp.full((nv, width), jnp.where(s == own + r, 0.5, 1.0), F32)
                    picked.append(win[step][s] * weight.astype(jnp.bfloat16))
                x = jnp.concatenate(picked, axis=1)
                w = jnp.concatenate([tiles[r, k] for k in range(kt)], axis=1)
                ahead[r] = lax.dot_general(x, w, ON_LAST, preferred_element_type=F32)
            return carry

        lax.fori_loop(0, FORWARD_PARTS, body, 0)

    for copy in smalls[3:]:
        copy.wait()
    center = center_s[0]
    inv = 1.0 / jnp.full((nv, width), half_s[0], F32)

    for step in range(2):
        if step == 0:
            tab_copy.wait()
        else:
            send_vectors(step)
        transposed_products(step)
        send_products(step)
        for g, copy, wanted in vector_hands(step):
            await_vectors(step, g)
            pl.when(wanted)(copy.start)
        for g in (1, 3):
            await_vectors(step, g)
        forward(step)
        pl.when(core == 0)(lambda: await_share(step, 2))
        scales = []
        for i in range(2):
            pl.when(exists(SPAN - 2 * i))(product_copy(step, i).wait_recv)
        for i in range(2):
            power = landed[step, i, rows].astype(jnp.int32).astype(F32)
            scales.append(jnp.exp2(power) * (1.0 / TOP))
        for r in range(rows):
            cut = slice(r * width, (r + 1) * width)
            v = ahead[r] + slot_sum(own + r) + shared[step, 2, r]
            for i in range(2):
                v = v + landed[step, i, r].astype(jnp.int32).astype(F32) * scales[i]
            (out1, out2)[step][:, cut] = v
            if step == 0:
                first = (v - center * win0[own + r].astype(F32)) * inv
                win1[own + r] = first.astype(jnp.bfloat16)

    for step in range(2):
        for wanted, copy in vector_sends(step):
            pl.when(wanted)(copy.wait_send)
        for g, copy, wanted in vector_hands(step):
            pl.when(wanted)(copy.wait_send)
        for i in range(2):
            share_copy(step, i).wait_send()
            pl.when(exists(2 * i - SPAN))(product_copy(step, i).wait_send)


def per_device(n, matrix_tiles, columns, vectors, center, halfwidth):
    rows, kt, width, _ = matrix_tiles.shape
    nv = vectors.shape[0]
    hbm = pl.BlockSpec(memory_space=pltpu.HBM)
    vmem = pl.BlockSpec(memory_space=pltpu.VMEM)
    out = jax.ShapeDtypeStruct(vectors.shape, F32)
    chain = rows // CHAINS * kt
    pinned = [
        pltpu.with_memory_space_constraint(a, pltpu.HBM)
        for a in (matrix_tiles, columns, vectors)
    ]
    one, two = pl.pallas_call(
        functools.partial(kernel, n),
        out_shape=(out, out),
        in_specs=[hbm] * 3 + [pl.BlockSpec(memory_space=pl.ANY)] * 2,
        out_specs=(vmem, vmem),
        scratch_shapes=[
            pltpu.VMEM(columns.shape, jnp.int32),
            pltpu.SMEM(columns.shape, jnp.int32),
            pltpu.VMEM(vectors.shape, jnp.bfloat16),
            pltpu.SMEM((1,), F32),
            pltpu.SMEM((1,), F32),
            pltpu.VMEM(matrix_tiles.shape, jnp.bfloat16),
            pltpu.VMEM(((SPAN + 1) * rows, nv, width), jnp.bfloat16),
            pltpu.VMEM(((SPAN + 1) * rows, nv, width), jnp.bfloat16),
            [pltpu.VMEM((chain + 1, nv, width), F32)] * CHAINS,
            pltpu.VMEM((rows, nv, width), F32),
            pltpu.VMEM((rows, nv, width), F32),
            pltpu.VMEM((2, 2, rows, nv, width), F32),
            pltpu.VMEM((2, 3, rows, nv, width), F32),
            pltpu.VMEM((2, 2, rows + 1, nv, width), jnp.int16),
            pltpu.VMEM((2, 2, rows + 1, nv, width), jnp.int16),
            pltpu.VMEM((SLOT_ROW + rows, 128), jnp.int32),
            pltpu.SMEM((SLOT_ROW + rows, 128), jnp.int32),
            pltpu.SemaphoreType.DMA((rows,)),
            pltpu.SemaphoreType.DMA((5,)),
            pltpu.SemaphoreType.DMA,
            pltpu.SemaphoreType.DMA((2, SPAN + 1)),
            pltpu.SemaphoreType.DMA((2, SPAN)),
            pltpu.SemaphoreType.DMA((2, 2)),
            pltpu.SemaphoreType.DMA((2, 3)),
            pltpu.SemaphoreType.DMA((2, 2)),
            pltpu.SemaphoreType.DMA((2, 2)),
        ],
        compiler_params=pltpu.CompilerParams(
            collective_id=0, has_side_effects=True, vmem_limit_bytes=32 << 20
        ),
    )(*pinned, center, halfwidth)
    initial = vectors.astype(F32)
    first = (one - center[0] * initial) / halfwidth[0]
    second = 2.0 * (two - center[0] * first) / halfwidth[0] - initial
    return first, second


def solution(mesh):
    placed = (P("tri", None, None, None), P("tri", None), P(None, "tri"), P(), P())
    return jax.shard_map(
        functools.partial(per_device, mesh.shape["tri"]),
        mesh=mesh,
        in_specs=placed,
        out_specs=(P(None, "tri"), P(None, "tri")),
        check_vma=False,
    )
```

```python
import functools

import jax
import jax.numpy as jnp
from jax import lax
from jax.experimental import pallas as pl
from jax.experimental.pallas import tpu as pltpu
from jax.sharding import PartitionSpec as P

SPAN = 4
BEHIND_PARTS = 2
FORWARD_PARTS = 2
CHAINS = 2
TOP = 32766.0
MESH = pl.DeviceIdType.MESH
F32 = jnp.float32
LAST_ROW = 16
SLOT_ROW = LAST_ROW + 8 * CHAINS


def kernel(
    n,
    tiles_hbm,
    cols_hbm,
    vec_hbm,
    center_hbm,
    half_hbm,
    out1,
    out2,
    shift,
    cols_v,
    cols_s,
    center_s,
    half_s,
    tiles,
    turned,
    win0,
    win1,
    blocks,
    sums,
    ahead,
    total,
    first,
    staged,
    shared,
    coded,
    landed,
    tab_v,
    tab_s,
    tile_sem,
    small_sem,
    tab_sem,
    xsend,
    xrecv,
    ssend,
    srecv,
    psend,
    precv,
):
    rows, kt, width, _ = tiles.shape
    nv, span = vec_hbm.shape
    half = rows // CHAINS
    none = half * kt
    me = lax.axis_index("tri")
    core = lax.rem(me, 2)
    other = me + 1 - 2 * core
    lowest = (me - SPAN) * rows

    def exists(d):
        return (me + d >= 0) & (me + d < n)


    def load(r):
        return pltpu.make_async_copy(tiles_hbm.at[r], tiles.at[r], tile_sem.at[r])

    def small(i, src, dst):
        return pltpu.make_async_copy(src, dst, small_sem.at[i])

    smalls = [
        small(0, cols_hbm, cols_s),
        small(1, cols_hbm, cols_v),
        small(2, vec_hbm, win0.at[:, pl.ds(SPAN * span, span)]),
        small(3, center_hbm, center_s),
        small(4, half_hbm, half_s),
    ]

    barrier = pltpu.get_barrier_semaphore()
    pl.semaphore_signal(barrier, inc=1, device_id=(other,), device_id_type=MESH)
    for d in (2, -2, 4, -4):

        @pl.when(exists(d))
        def _():
            pl.semaphore_signal(barrier, inc=1, device_id=(me + d,), device_id_type=MESH)

    for copy in smalls:
        copy.start()
    for j in range(half):
        for c in range(CHAINS):
            load(c * half + j).start()
    own = SPAN * rows
    win = (win0, win1)

    def block(s):
        return pl.ds(pl.multiple_of(s * width, width), width)

    for i, d in enumerate((4, 2)):

        @pl.when(jnp.logical_not(exists(d)))
        def _():
            for step in range(2):
                landed[step, i] = jnp.zeros(landed.shape[2:], landed.dtype)

    for step in range(2):
        shared[step, 2 * core] = jnp.zeros(shared.shape[2:], F32)


    def vector_copy(step, i, src, dst, to):
        from_hbm = step == 0 and src == SPAN
        return pltpu.make_async_remote_copy(
            src_ref=vec_hbm if from_hbm else win[step].at[:, pl.ds(src * span, span)],
            dst_ref=win[step].at[:, pl.ds(pl.multiple_of(dst * span, span), span)],
            send_sem=xsend.at[step, i],
            recv_sem=xrecv.at[step, dst],
            device_id=(to,),
            device_id_type=MESH,
        )

    def vector_sends(step):
        far = vector_copy(step, 1, SPAN, SPAN - 4, me + 4)
        return [
            (core == 0, vector_copy(step, 0, SPAN, SPAN - 1, other)),
            (exists(4) & (core == 1), far),
            (exists(2), vector_copy(step, 2, SPAN, SPAN - 2, me + 2)),
            (exists(4) & (core == 0), far),
        ]

    def vector_hands(step):
        return [
            (2, vector_copy(step, 3, 2, 1 + 2 * core, other), exists(-2)),
            (0, vector_copy(step, 4, 0, 1, other), exists(-4) & (core == 1)),
        ]

    def await_vectors(step, g):
        @pl.when(exists(g - SPAN))
        def _():
            vector_copy(step, 0, SPAN, g, other).wait_recv()

    def send_vectors(step):
        for wanted, copy in vector_sends(step):
            pl.when(wanted)(copy.start)

    for c in range(CHAINS):
        sums[c][none] = jnp.zeros((nv, width), F32)
    for copy in smalls[:2]:
        copy.wait()
    tid = lax.broadcasted_iota(jnp.int32, (half, kt), 0) * kt + lax.broadcasted_iota(
        jnp.int32, (half, kt), 1
    )
    lane = lax.broadcasted_iota(jnp.int32, (8, 128), 1)
    slots = jnp.clip(cols_v[...] - lowest, 0, (SPAN + 1) * rows - 1)
    tab_v[SLOT_ROW : SLOT_ROW + rows, 0:kt] = slots
    for c in range(CHAINS):
        mine = slots[c * half : (c + 1) * half]

        def note(j, carry):
            prev, last = carry
            for k in range(kt):
                s = cols_s[c * half + j, k] - lowest
                t = j * kt + k
                prev = jnp.where((mine == s) & (tid > t), t, prev)
                last = jnp.where(lane == s, t, last)
            return prev, last

        prev, last = lax.fori_loop(
            0,
            half,
            note,
            (jnp.full((half, kt), none, jnp.int32), jnp.full((8, 128), none, jnp.int32)),
        )
        tab_v[c * half : (c + 1) * half, 0:kt] = prev
        tab_v[LAST_ROW + 8 * c : LAST_ROW + 8 * (c + 1), :] = last
    tab_copy = pltpu.make_async_copy(tab_v, tab_s, tab_sem)
    tab_copy.start()

    def share_copy(step, i):
        return pltpu.make_async_remote_copy(
            src_ref=staged.at[step, i],
            dst_ref=shared.at[step, core + i],
            send_sem=ssend.at[step, i],
            recv_sem=srecv.at[step, core + i],
            device_id=(other,),
            device_id_type=MESH,
        )

    def await_share(step, i):
        pltpu.make_async_remote_copy(
            src_ref=staged.at[step, 0],
            dst_ref=shared.at[step, i],
            send_sem=ssend.at[step, 0],
            recv_sem=srecv.at[step, i],
            device_id=(other,),
            device_id_type=MESH,
        ).wait_recv()

    def product_copy(step, i):
        return pltpu.make_async_remote_copy(
            src_ref=coded.at[step, i],
            dst_ref=landed.at[step, i],
            send_sem=psend.at[step, i],
            recv_sem=precv.at[step, i],
            device_id=(me - SPAN + 2 * i,),
            device_id_type=MESH,
        )

    def transposed_products(step):
        def body(part, carry):
            for i in range(half // BEHIND_PARTS):
                j = part * (half // BEHIND_PARTS) + i
                if step == 0:
                    for c in range(CHAINS):
                        load(c * half + j).wait()
                for k in range(0, kt, 2):
                    for c in range(CHAINS):
                        add_pair(step, c, j, k)
            return carry

        lax.fori_loop(0, BEHIND_PARTS, body, 0)

    def add_pair(step, c, j, k):
        r = c * half + j
        pair = jnp.concatenate([tiles[r, k], tiles[r, k + 1]], axis=1)
        both = jnp.dot(win[step][:, block(own + r)], pair, preferred_element_type=F32)
        for i in range(2):
            slot = tab_s[SLOT_ROW + r, k + i]
            weight = jnp.where(slot == own + r, 0.5, 1.0).astype(F32)
            part = both[:, i * width : (i + 1) * width] * weight
            before = tab_s[r, k + i]
            sums[c][j * kt + k + i] = part + sums[c][before]

    def slot_sum(s):
        return sum(sums[c][tab_s[LAST_ROW + 8 * c, s]] for c in range(CHAINS))

    def stage_products(step):
        for i in range(2):
            for r in range(rows):
                staged[step, i, r] = slot_sum((2 * i + 1) * rows + r)

    def send_products(step):
        for i in range(2):
            share_copy(step, i).start()
        for i in range(2):
            if i == 0:
                pl.when(core == 1)(lambda: await_share(step, 0))
            else:
                await_share(step, 1)
            most = jnp.zeros((nv, width), F32)
            for r in range(rows):
                v = slot_sum(2 * i * rows + r) + shared[step, i, r]
                total[r] = v
                most = jnp.maximum(most, jnp.abs(v))
            peak = jnp.maximum(jnp.max(most, axis=1, keepdims=True), 1e-30)
            power = jnp.broadcast_to(jnp.ceil(jnp.log2(peak)), (nv, width))
            scale = jnp.exp2(-power) * TOP
            for r in range(rows):
                coded[step, i, r] = (
                    jnp.round(total[r] * scale).astype(jnp.int32).astype(jnp.int16)
                )
            coded[step, i, rows] = power.astype(jnp.int32).astype(jnp.int16)
            pl.when(exists(2 * i - SPAN))(product_copy(step, i).start)

    def turn():
        def body(r, carry):
            for k in range(kt):
                turned[r, k * width : (k + 1) * width, :] = tiles[r, k].T
            return carry

        lax.fori_loop(0, rows, body, 0)

    def forward(step):
        for s in range(own + rows):
            blocks[s] = win[step][:, block(s)]

        def body(part, carry):
            for i in range(rows // FORWARD_PARTS):
                r = part * (rows // FORWARD_PARTS) + i
                picked = []
                for k in range(kt):
                    slot = tab_s[SLOT_ROW + r, k]
                    weight = jnp.full((nv, width), jnp.where(slot == own + r, 0.5, 1.0), F32)
                    picked.append(blocks[slot] * weight.astype(jnp.bfloat16))
                x = jnp.concatenate(picked, axis=1)
                ahead[r] = jnp.dot(x, turned[r], preferred_element_type=F32)
            return carry

        lax.fori_loop(0, FORWARD_PARTS, body, 0)

    for copy in smalls[3:]:
        copy.wait()
    center = center_s[0]
    inv = 1.0 / jnp.full((nv, width), half_s[0], F32)

    shift[...] = jnp.broadcast_to((center * inv)[:1, :1], shift.shape)

    greeted = 1 + jnp.minimum(me // 2, 2) + jnp.minimum((n - 1 - me) // 2, 2)
    for step in range(2):
        if step == 0:
            tab_copy.wait()
            smalls[2].wait()
        else:
            send_vectors(step)
        transposed_products(step)
        stage_products(step)
        if step == 0:
            pl.semaphore_wait(barrier, greeted)
            send_vectors(step)
        send_products(step)
        if step == 0:
            turn()
        for g, copy, wanted in vector_hands(step):
            await_vectors(step, g)
            pl.when(wanted)(copy.start)
        for g in (1, 3):
            await_vectors(step, g)
        forward(step)
        pl.when(core == 0)(lambda: await_share(step, 2))
        scales = []
        for i in range(2):
            pl.when(exists(SPAN - 2 * i))(product_copy(step, i).wait_recv)
        for i in range(2):
            power = landed[step, i, rows].astype(jnp.int32).astype(F32)
            scales.append(jnp.exp2(power) * (1.0 / TOP))
        for r in range(rows):
            cut = slice(r * width, (r + 1) * width)
            v = ahead[r] + slot_sum(own + r) + shared[step, 2, r]
            for i in range(2):
                v = v + landed[step, i, r].astype(jnp.int32).astype(F32) * scales[i]
            if step == 0:
                out1[:, cut] = v * inv
                first[r] = v * inv - win0[:, block(own + r)].astype(F32) * (center * inv)
                win1[:, block(own + r)] = first[r].astype(jnp.bfloat16)
            else:
                out2[:, cut] = 2.0 * (v - center * first[r]) * inv

    for step in range(2):
        for wanted, copy in vector_sends(step):
            pl.when(wanted)(copy.wait_send)
        for g, copy, wanted in vector_hands(step):
            pl.when(wanted)(copy.wait_send)
        for i in range(2):
            share_copy(step, i).wait_send()
            pl.when(exists(2 * i - SPAN))(product_copy(step, i).wait_send)


def per_device(n, matrix_tiles, columns, vectors, center, halfwidth):
    rows, kt, width, _ = matrix_tiles.shape
    nv = vectors.shape[0]
    hbm = pl.BlockSpec(memory_space=pltpu.HBM)
    vmem = pl.BlockSpec(memory_space=pltpu.VMEM)
    out = jax.ShapeDtypeStruct(vectors.shape, F32)
    chain = rows // CHAINS * kt
    pinned = [
        pltpu.with_memory_space_constraint(a, pltpu.HBM)
        for a in (matrix_tiles, columns, vectors)
    ]
    one, two, shift = pl.pallas_call(
        functools.partial(kernel, n),
        out_shape=(out, out, jax.ShapeDtypeStruct((1, vectors.shape[1]), F32)),
        in_specs=[hbm] * 3 + [pl.BlockSpec(memory_space=pl.ANY)] * 2,
        out_specs=(vmem, vmem, vmem),
        scratch_shapes=[
            pltpu.VMEM(columns.shape, jnp.int32),
            pltpu.SMEM(columns.shape, jnp.int32),
            pltpu.SMEM((1,), F32),
            pltpu.SMEM((1,), F32),
            pltpu.VMEM(matrix_tiles.shape, jnp.bfloat16),
            pltpu.VMEM((rows, kt * width, width), jnp.bfloat16),
            pltpu.VMEM((nv, (SPAN + 1) * vectors.shape[1]), jnp.bfloat16),
            pltpu.VMEM((nv, (SPAN + 1) * vectors.shape[1]), jnp.bfloat16),
            pltpu.VMEM(((SPAN + 1) * rows, nv, width), jnp.bfloat16),
            [pltpu.VMEM((chain + 1, nv, width), F32)] * CHAINS,
            pltpu.VMEM((rows, nv, width), F32),
            pltpu.VMEM((rows, nv, width), F32),
            pltpu.VMEM((rows, nv, width), F32),
            pltpu.VMEM((2, 2, rows, nv, width), F32),
            pltpu.VMEM((2, 3, rows, nv, width), F32),
            pltpu.VMEM((2, 2, rows + 1, nv, width), jnp.int16),
            pltpu.VMEM((2, 2, rows + 1, nv, width), jnp.int16),
            pltpu.VMEM((SLOT_ROW + rows, 128), jnp.int32),
            pltpu.SMEM((SLOT_ROW + rows, 128), jnp.int32),
            pltpu.SemaphoreType.DMA((rows,)),
            pltpu.SemaphoreType.DMA((5,)),
            pltpu.SemaphoreType.DMA,
            pltpu.SemaphoreType.DMA((2, SPAN + 1)),
            pltpu.SemaphoreType.DMA((2, SPAN)),
            pltpu.SemaphoreType.DMA((2, 2)),
            pltpu.SemaphoreType.DMA((2, 3)),
            pltpu.SemaphoreType.DMA((2, 2)),
            pltpu.SemaphoreType.DMA((2, 2)),
        ],
        compiler_params=pltpu.CompilerParams(
            collective_id=0, has_side_effects=True, vmem_limit_bytes=32 << 20
        ),
    )(*pinned, center, halfwidth)
    initial = vectors.astype(F32)
    return one - initial * shift, two - initial


def solution(mesh):
    placed = (P("tri", None, None, None), P("tri", None), P(None, "tri"), P(), P())
    return jax.shard_map(
        functools.partial(per_device, mesh.shape["tri"]),
        mesh=mesh,
        in_specs=placed,
        out_specs=(P(None, "tri"), P(None, "tri")),
        check_vma=False,
    )
```

```python
import functools

import jax
import jax.numpy as jnp
from jax import lax
from jax.experimental import pallas as pl
from jax.experimental.pallas import tpu as pltpu
from jax.sharding import PartitionSpec as P

SPAN = 4
BEHIND_PARTS = 2
FORWARD_PARTS = 2
LINE = 8
CHAINS = 2
TOP = 32766.0
MESH = pl.DeviceIdType.MESH
F32 = jnp.float32
LAST_ROW = 16
SLOT_ROW = LAST_ROW + 8 * CHAINS


def kernel(
    n,
    tiles_hbm,
    cols_hbm,
    vec_hbm,
    center_hbm,
    half_hbm,
    out1,
    out2,
    shift,
    cols_v,
    cols_s,
    center_s,
    half_s,
    tiles,
    turned,
    win0,
    win1,
    blocks,
    sums,
    ahead,
    total,
    first,
    staged,
    shared,
    coded,
    landed,
    relayed,
    tab_v,
    tab_s,
    tile_sem,
    small_sem,
    tab_sem,
    xsend,
    xrecv,
    ssend,
    srecv,
    psend,
    precv,
    rrecv,
):
    rows, kt, width, _ = tiles.shape
    nv, span = vec_hbm.shape
    half = rows // CHAINS
    none = half * kt
    me = lax.axis_index("tri")
    chip = lax.rem(me // 2, LINE)

    def exists(d):
        return (me + d >= 0) & (me + d < n)


    core = lax.rem(me, 2)
    relays = (chip == 1) & exists(-4)
    gathers = (chip == 0) & exists(-2)
    goes = (exists(-4) & (chip != 1), exists(-2))
    comes = (exists(4) & (chip != LINE - 1), exists(2))
    other = me + 1 - 2 * core
    lowest = (me - SPAN) * rows

    def load(r):
        return pltpu.make_async_copy(tiles_hbm.at[r], tiles.at[r], tile_sem.at[r])

    def small(i, src, dst):
        return pltpu.make_async_copy(src, dst, small_sem.at[i])

    smalls = [
        small(0, cols_hbm, cols_s),
        small(1, cols_hbm, cols_v),
        small(2, vec_hbm, win0.at[:, pl.ds(SPAN * span, span)]),
        small(3, center_hbm, center_s),
        small(4, half_hbm, half_s),
    ]

    barrier = pltpu.get_barrier_semaphore()
    pl.semaphore_signal(barrier, inc=1, device_id=(other,), device_id_type=MESH)
    for d, wanted in ((2, comes[1]), (-2, exists(-2)), (4, comes[0]), (-4, exists(-4))):

        @pl.when(wanted)
        def _():
            pl.semaphore_signal(barrier, inc=1, device_id=(me + d,), device_id_type=MESH)

    for copy in smalls:
        copy.start()
    for j in range(half):
        for c in range(CHAINS):
            load(c * half + j).start()
    own = SPAN * rows
    win = (win0, win1)

    def block(s):
        return pl.ds(pl.multiple_of(s * width, width), width)

    for i in range(2):

        @pl.when(jnp.logical_not(comes[i]))
        def _():
            for step in range(2):
                landed[step, i] = jnp.zeros(landed.shape[2:], landed.dtype)

    @pl.when(jnp.logical_not(gathers))
    def _():
        relayed[...] = jnp.zeros(relayed.shape, relayed.dtype)

    for step in range(2):
        shared[step, 2 * core] = jnp.zeros(shared.shape[2:], F32)


    def vector_copy(step, i, src, dst, to):
        from_hbm = step == 0 and src == SPAN
        return pltpu.make_async_remote_copy(
            src_ref=vec_hbm if from_hbm else win[step].at[:, pl.ds(src * span, span)],
            dst_ref=win[step].at[:, pl.ds(pl.multiple_of(dst * span, span), span)],
            send_sem=xsend.at[step, i],
            recv_sem=xrecv.at[step, dst],
            device_id=(to,),
            device_id_type=MESH,
        )

    far_first = jnp.where(chip >= LINE - 2, chip == LINE - 2, core == 1)

    def vector_sends(step):
        far = vector_copy(step, 1, SPAN, SPAN - 4, me + 4)
        return [
            (core == 0, vector_copy(step, 0, SPAN, SPAN - 1, other)),
            (exists(4) & far_first, far),
            (exists(2), vector_copy(step, 2, SPAN, SPAN - 2, me + 2)),
            (exists(4) & jnp.logical_not(far_first), far),
        ]

    def vector_hands(step):
        return [
            (2, vector_copy(step, 3, 2, 1 + 2 * core, other), exists(-2)),
            (0, vector_copy(step, 4, 0, 1, other), exists(-4) & (core == 1)),
        ]

    def await_vectors(step, g):
        @pl.when(exists(g - SPAN))
        def _():
            vector_copy(step, 0, SPAN, g, other).wait_recv()

    def send_vectors(step):
        for wanted, copy in vector_sends(step):
            pl.when(wanted)(copy.start)

    for c in range(CHAINS):
        sums[c][none] = jnp.zeros((nv, width), F32)
    for copy in smalls[:2]:
        copy.wait()
    tid = lax.broadcasted_iota(jnp.int32, (half, kt), 0) * kt + lax.broadcasted_iota(
        jnp.int32, (half, kt), 1
    )
    lane = lax.broadcasted_iota(jnp.int32, (8, 128), 1)
    slots = jnp.clip(cols_v[...] - lowest, 0, (SPAN + 1) * rows - 1)
    tab_v[SLOT_ROW : SLOT_ROW + rows, 0:kt] = slots
    for c in range(CHAINS):
        mine = slots[c * half : (c + 1) * half]

        def note(j, carry):
            prev, last = carry
            for k in range(kt):
                s = cols_s[c * half + j, k] - lowest
                t = j * kt + k
                prev = jnp.where((mine == s) & (tid > t), t, prev)
                last = jnp.where(lane == s, t, last)
            return prev, last

        prev, last = lax.fori_loop(
            0,
            half,
            note,
            (jnp.full((half, kt), none, jnp.int32), jnp.full((8, 128), none, jnp.int32)),
        )
        tab_v[c * half : (c + 1) * half, 0:kt] = prev
        tab_v[LAST_ROW + 8 * c : LAST_ROW + 8 * (c + 1), :] = last
    tab_copy = pltpu.make_async_copy(tab_v, tab_s, tab_sem)
    tab_copy.start()

    def share_copy(step, i):
        return pltpu.make_async_remote_copy(
            src_ref=staged.at[step, i],
            dst_ref=shared.at[step, core + i],
            send_sem=ssend.at[step, i],
            recv_sem=srecv.at[step, core + i],
            device_id=(other,),
            device_id_type=MESH,
        )

    def await_share(step, i):
        pltpu.make_async_remote_copy(
            src_ref=staged.at[step, 0],
            dst_ref=shared.at[step, i],
            send_sem=ssend.at[step, 0],
            recv_sem=srecv.at[step, i],
            device_id=(other,),
            device_id_type=MESH,
        ).wait_recv()

    def product_copy(step, i):
        return pltpu.make_async_remote_copy(
            src_ref=coded.at[step, i],
            dst_ref=landed.at[step, i],
            send_sem=psend.at[step, i],
            recv_sem=precv.at[step, i],
            device_id=(me - SPAN + 2 * i,),
            device_id_type=MESH,
        )

    def relay_copy(step):
        return pltpu.make_async_remote_copy(
            src_ref=coded.at[step, 0],
            dst_ref=relayed.at[step],
            send_sem=psend.at[step, 0],
            recv_sem=rrecv.at[step],
            device_id=(me - 2,),
            device_id_type=MESH,
        )

    def transposed_products(step):
        def body(part, carry):
            for i in range(half // BEHIND_PARTS):
                j = part * (half // BEHIND_PARTS) + i
                if step == 0:
                    for c in range(CHAINS):
                        load(c * half + j).wait()
                for k in range(0, kt, 2):
                    for c in range(CHAINS):
                        add_pair(step, c, j, k)
            return carry

        lax.fori_loop(0, BEHIND_PARTS, body, 0)

    def add_pair(step, c, j, k):
        r = c * half + j
        pair = jnp.concatenate([tiles[r, k], tiles[r, k + 1]], axis=1)
        both = jnp.dot(win[step][:, block(own + r)], pair, preferred_element_type=F32)
        for i in range(2):
            slot = tab_s[SLOT_ROW + r, k + i]
            weight = jnp.where(slot == own + r, 0.5, 1.0).astype(F32)
            part = both[:, i * width : (i + 1) * width] * weight
            before = tab_s[r, k + i]
            sums[c][j * kt + k + i] = part + sums[c][before]

    def slot_sum(s):
        return sum(sums[c][tab_s[LAST_ROW + 8 * c, s]] for c in range(CHAINS))

    def stage_products(step):
        for i in range(2):
            for r in range(rows):
                staged[step, i, r] = slot_sum((2 * i + 1) * rows + r)

    def send_products(step):
        for i in range(2):
            share_copy(step, i).start()
        for i in range(2):
            if i == 0:
                pl.when(core == 1)(lambda: await_share(step, 0))
            else:
                await_share(step, 1)
                pl.when(gathers)(relay_copy(step).wait_recv)
                power = relayed[step, rows].astype(jnp.int32).astype(F32)
                unit = jnp.exp2(power) * (1.0 / TOP)
            most = jnp.zeros((nv, width), F32)
            for r in range(rows):
                v = slot_sum(2 * i * rows + r) + shared[step, i, r]
                if i == 1:
                    v = v + relayed[step, r].astype(jnp.int32).astype(F32) * unit
                total[r] = v
                most = jnp.maximum(most, jnp.abs(v))
            peak = jnp.maximum(jnp.max(most, axis=1, keepdims=True), 1e-30)
            power = jnp.broadcast_to(jnp.ceil(jnp.log2(peak)), (nv, width))
            scale = jnp.exp2(-power) * TOP
            for r in range(rows):
                coded[step, i, r] = (
                    jnp.round(total[r] * scale).astype(jnp.int32).astype(jnp.int16)
                )
            coded[step, i, rows] = power.astype(jnp.int32).astype(jnp.int16)
            pl.when(goes[i])(product_copy(step, i).start)
            if i == 0:
                pl.when(relays)(relay_copy(step).start)

    def turn():
        def body(r, carry):
            for k in range(kt):
                turned[r, k * width : (k + 1) * width, :] = tiles[r, k].T
            return carry

        lax.fori_loop(0, rows, body, 0)

    def forward(step):
        for s in range(own + rows):
            blocks[s] = win[step][:, block(s)]

        def body(part, carry):
            for i in range(rows // FORWARD_PARTS):
                r = part * (rows // FORWARD_PARTS) + i
                picked = []
                for k in range(kt):
                    slot = tab_s[SLOT_ROW + r, k]
                    weight = jnp.full((nv, width), jnp.where(slot == own + r, 0.5, 1.0), F32)
                    picked.append(blocks[slot] * weight.astype(jnp.bfloat16))
                x = jnp.concatenate(picked, axis=1)
                ahead[r] = jnp.dot(x, turned[r], preferred_element_type=F32)
            return carry

        lax.fori_loop(0, FORWARD_PARTS, body, 0)

    for copy in smalls[3:]:
        copy.wait()
    center = center_s[0]
    inv = 1.0 / jnp.full((nv, width), half_s[0], F32)

    shift[...] = jnp.broadcast_to((center * inv)[:1, :1], shift.shape)

    greeted = 1 + jnp.minimum(me // 2, 2) + jnp.minimum((n - 1 - me) // 2, 2)
    greeted = greeted - jnp.where(relays, 1, 0)
    def enter():
        pl.semaphore_wait(barrier, greeted)
        send_vectors(0)

    for step in range(2):
        if step == 0:
            tab_copy.wait()
            smalls[2].wait()

            @pl.when(chip >= LINE - 2)
            def _():
                enter()
        else:
            send_vectors(step)
        transposed_products(step)
        stage_products(step)
        if step == 0:

            @pl.when(chip < LINE - 2)
            def _():
                enter()
        send_products(step)
        if step == 0:
            turn()
        for g, copy, wanted in vector_hands(step):
            await_vectors(step, g)
            pl.when(wanted)(copy.start)
        for g in (1, 3):
            await_vectors(step, g)
        forward(step)
        pl.when(core == 0)(lambda: await_share(step, 2))
        scales = []
        for i in range(2):
            pl.when(comes[i])(product_copy(step, i).wait_recv)
        for i in range(2):
            power = landed[step, i, rows].astype(jnp.int32).astype(F32)
            scales.append(jnp.exp2(power) * (1.0 / TOP))
        for r in range(rows):
            cut = slice(r * width, (r + 1) * width)
            v = ahead[r] + slot_sum(own + r) + shared[step, 2, r]
            for i in range(2):
                v = v + landed[step, i, r].astype(jnp.int32).astype(F32) * scales[i]
            if step == 0:
                out1[:, cut] = v * inv
                first[r] = v * inv - win0[:, block(own + r)].astype(F32) * (center * inv)
                win1[:, block(own + r)] = first[r].astype(jnp.bfloat16)
            else:
                out2[:, cut] = 2.0 * (v - center * first[r]) * inv

    for step in range(2):
        for wanted, copy in vector_sends(step):
            pl.when(wanted)(copy.wait_send)
        for g, copy, wanted in vector_hands(step):
            pl.when(wanted)(copy.wait_send)
        for i in range(2):
            share_copy(step, i).wait_send()
            pl.when(goes[i])(product_copy(step, i).wait_send)
        pl.when(relays)(relay_copy(step).wait_send)


def per_device(n, matrix_tiles, columns, vectors, center, halfwidth):
    rows, kt, width, _ = matrix_tiles.shape
    nv = vectors.shape[0]
    hbm = pl.BlockSpec(memory_space=pltpu.HBM)
    vmem = pl.BlockSpec(memory_space=pltpu.VMEM)
    out = jax.ShapeDtypeStruct(vectors.shape, F32)
    chain = rows // CHAINS * kt
    pinned = [
        pltpu.with_memory_space_constraint(a, pltpu.HBM)
        for a in (matrix_tiles, columns, vectors)
    ]
    one, two, shift = pl.pallas_call(
        functools.partial(kernel, n),
        out_shape=(out, out, jax.ShapeDtypeStruct((1, vectors.shape[1]), F32)),
        in_specs=[hbm] * 3 + [pl.BlockSpec(memory_space=pl.ANY)] * 2,
        out_specs=(vmem, vmem, vmem),
        scratch_shapes=[
            pltpu.VMEM(columns.shape, jnp.int32),
            pltpu.SMEM(columns.shape, jnp.int32),
            pltpu.SMEM((1,), F32),
            pltpu.SMEM((1,), F32),
            pltpu.VMEM(matrix_tiles.shape, jnp.bfloat16),
            pltpu.VMEM((rows, kt * width, width), jnp.bfloat16),
            pltpu.VMEM((nv, (SPAN + 1) * vectors.shape[1]), jnp.bfloat16),
            pltpu.VMEM((nv, (SPAN + 1) * vectors.shape[1]), jnp.bfloat16),
            pltpu.VMEM(((SPAN + 1) * rows, nv, width), jnp.bfloat16),
            [pltpu.VMEM((chain + 1, nv, width), F32)] * CHAINS,
            pltpu.VMEM((rows, nv, width), F32),
            pltpu.VMEM((rows, nv, width), F32),
            pltpu.VMEM((rows, nv, width), F32),
            pltpu.VMEM((2, 2, rows, nv, width), F32),
            pltpu.VMEM((2, 3, rows, nv, width), F32),
            pltpu.VMEM((2, 2, rows + 1, nv, width), jnp.int16),
            pltpu.VMEM((2, 2, rows + 1, nv, width), jnp.int16),
            pltpu.VMEM((2, rows + 1, nv, width), jnp.int16),
            pltpu.VMEM((SLOT_ROW + rows, 128), jnp.int32),
            pltpu.SMEM((SLOT_ROW + rows, 128), jnp.int32),
            pltpu.SemaphoreType.DMA((rows,)),
            pltpu.SemaphoreType.DMA((5,)),
            pltpu.SemaphoreType.DMA,
            pltpu.SemaphoreType.DMA((2, SPAN + 1)),
            pltpu.SemaphoreType.DMA((2, SPAN)),
            pltpu.SemaphoreType.DMA((2, 2)),
            pltpu.SemaphoreType.DMA((2, 3)),
            pltpu.SemaphoreType.DMA((2, 2)),
            pltpu.SemaphoreType.DMA((2, 2)),
            pltpu.SemaphoreType.DMA((2,)),
        ],
        compiler_params=pltpu.CompilerParams(
            collective_id=0, has_side_effects=True, vmem_limit_bytes=32 << 20
        ),
    )(*pinned, center, halfwidth)
    initial = vectors.astype(F32)
    return one - initial * shift, two - initial


def solution(mesh):
    placed = (P("tri", None, None, None), P("tri", None), P(None, "tri"), P(), P())
    return jax.shard_map(
        functools.partial(per_device, mesh.shape["tri"]),
        mesh=mesh,
        in_specs=placed,
        out_specs=(P(None, "tri"), P(None, "tri")),
        check_vma=False,
    )
```

```python
import functools

import jax
import jax.numpy as jnp
from jax import lax
from jax.experimental import pallas as pl
from jax.experimental.pallas import tpu as pltpu
from jax.sharding import PartitionSpec as P

SPAN = 4
BEHIND_PARTS = 2
FORWARD_PARTS = 2
LINE = 8
CHAINS = 2
TOP = 32766.0
MESH = pl.DeviceIdType.MESH
F32 = jnp.float32
LAST_ROW = 16
SLOT_ROW = LAST_ROW + 8 * CHAINS


def kernel(
    n,
    tiles_hbm,
    cols_hbm,
    vec_hbm,
    center_hbm,
    half_hbm,
    out1,
    out2,
    shift,
    cols_v,
    cols_s,
    center_s,
    half_s,
    tiles,
    turned,
    win0,
    win1,
    blocks,
    sums,
    ahead,
    total,
    first,
    staged,
    shared,
    coded,
    landed,
    relayed,
    tab_v,
    tab_s,
    tile_sem,
    small_sem,
    tab_sem,
    xsend,
    xrecv,
    ssend,
    srecv,
    psend,
    precv,
    rrecv,
):
    rows, kt, width, _ = tiles.shape
    nv, span = vec_hbm.shape
    half = rows // CHAINS
    none = half * kt
    me = lax.axis_index("tri")
    chip = lax.rem(me // 2, LINE)

    def exists(d):
        return (me + d >= 0) & (me + d < n)


    core = lax.rem(me, 2)
    relays = (chip == 1) & exists(-4)
    gathers = (chip == 0) & exists(-2)
    goes = (exists(-4) & (chip != 1), exists(-2))
    comes = (exists(4) & (chip != LINE - 1), exists(2))
    other = me + 1 - 2 * core
    lowest = (me - SPAN) * rows

    def load(r):
        return pltpu.make_async_copy(tiles_hbm.at[r], tiles.at[r], tile_sem.at[r])

    def small(i, src, dst):
        return pltpu.make_async_copy(src, dst, small_sem.at[i])

    smalls = [
        small(0, cols_hbm, cols_s),
        small(1, cols_hbm, cols_v),
        small(2, vec_hbm, win0.at[:, pl.ds(SPAN * span, span)]),
        small(3, center_hbm, center_s),
        small(4, half_hbm, half_s),
    ]

    barrier = pltpu.get_barrier_semaphore()
    pl.semaphore_signal(barrier, inc=1, device_id=(other,), device_id_type=MESH)
    for d, wanted in ((2, comes[1]), (-2, exists(-2)), (4, comes[0]), (-4, exists(-4))):

        @pl.when(wanted)
        def _():
            pl.semaphore_signal(barrier, inc=1, device_id=(me + d,), device_id_type=MESH)

    for copy in smalls:
        copy.start()
    for j in range(half):
        for c in range(CHAINS):
            load(c * half + j).start()
    own = SPAN * rows
    win = (win0, win1)

    def block(s):
        return pl.ds(pl.multiple_of(s * width, width), width)

    for i in range(2):

        @pl.when(jnp.logical_not(comes[i]))
        def _():
            for step in range(2):
                landed[step, i] = jnp.zeros(landed.shape[2:], landed.dtype)

    @pl.when(jnp.logical_not(gathers))
    def _():
        relayed[...] = jnp.zeros(relayed.shape, relayed.dtype)

    for step in range(2):
        shared[step, 2 * core] = jnp.zeros(shared.shape[2:], F32)


    def vector_copy(step, i, src, dst, to):
        from_hbm = step == 0 and src == SPAN
        return pltpu.make_async_remote_copy(
            src_ref=vec_hbm if from_hbm else win[step].at[:, pl.ds(src * span, span)],
            dst_ref=win[step].at[:, pl.ds(pl.multiple_of(dst * span, span), span)],
            send_sem=xsend.at[step, i],
            recv_sem=xrecv.at[step, dst],
            device_id=(to,),
            device_id_type=MESH,
        )

    far_first = jnp.where(chip >= LINE - 2, chip == LINE - 2, core == 1)

    def vector_sends(step):
        far = vector_copy(step, 1, SPAN, SPAN - 4, me + 4)
        return [
            (core == 0, vector_copy(step, 0, SPAN, SPAN - 1, other)),
            (exists(4) & far_first, far),
            (exists(2), vector_copy(step, 2, SPAN, SPAN - 2, me + 2)),
            (exists(4) & jnp.logical_not(far_first), far),
        ]

    def vector_hands(step):
        return [
            (2, vector_copy(step, 3, 2, 1 + 2 * core, other), exists(-2)),
            (0, vector_copy(step, 4, 0, 1, other), exists(-4) & (core == 1)),
        ]

    def await_vectors(step, g):
        @pl.when(exists(g - SPAN))
        def _():
            vector_copy(step, 0, SPAN, g, other).wait_recv()

    def send_vectors(step):
        for wanted, copy in vector_sends(step):
            pl.when(wanted)(copy.start)

    for c in range(CHAINS):
        sums[c][none] = jnp.zeros((nv, width), F32)
    for copy in smalls[:2]:
        copy.wait()
    tid = lax.broadcasted_iota(jnp.int32, (half, kt), 0) * kt + lax.broadcasted_iota(
        jnp.int32, (half, kt), 1
    )
    lane = lax.broadcasted_iota(jnp.int32, (8, 128), 1)
    slots = jnp.clip(cols_v[...] - lowest, 0, (SPAN + 1) * rows - 1)
    tab_v[SLOT_ROW : SLOT_ROW + rows, 0:kt] = slots
    for c in range(CHAINS):
        mine = slots[c * half : (c + 1) * half]

        def note(j, carry):
            prev, last = carry
            for k in range(kt):
                s = cols_s[c * half + j, k] - lowest
                t = j * kt + k
                prev = jnp.where((mine == s) & (tid > t), t, prev)
                last = jnp.where(lane == s, t, last)
            return prev, last

        prev, last = lax.fori_loop(
            0,
            half,
            note,
            (jnp.full((half, kt), none, jnp.int32), jnp.full((8, 128), none, jnp.int32)),
        )
        tab_v[c * half : (c + 1) * half, 0:kt] = prev
        tab_v[LAST_ROW + 8 * c : LAST_ROW + 8 * (c + 1), :] = last
    tab_copy = pltpu.make_async_copy(tab_v, tab_s, tab_sem)
    tab_copy.start()

    def share_copy(step, i):
        return pltpu.make_async_remote_copy(
            src_ref=staged.at[step, i],
            dst_ref=shared.at[step, core + i],
            send_sem=ssend.at[step, i],
            recv_sem=srecv.at[step, core + i],
            device_id=(other,),
            device_id_type=MESH,
        )

    def await_share(step, i):
        pltpu.make_async_remote_copy(
            src_ref=staged.at[step, 0],
            dst_ref=shared.at[step, i],
            send_sem=ssend.at[step, 0],
            recv_sem=srecv.at[step, i],
            device_id=(other,),
            device_id_type=MESH,
        ).wait_recv()

    def product_copy(step, i):
        return pltpu.make_async_remote_copy(
            src_ref=coded.at[step, i],
            dst_ref=landed.at[step, i],
            send_sem=psend.at[step, i],
            recv_sem=precv.at[step, i],
            device_id=(me - SPAN + 2 * i,),
            device_id_type=MESH,
        )

    def relay_copy(step):
        return pltpu.make_async_remote_copy(
            src_ref=coded.at[step, 0],
            dst_ref=relayed.at[step],
            send_sem=psend.at[step, 0],
            recv_sem=rrecv.at[step],
            device_id=(me - 2,),
            device_id_type=MESH,
        )

    def transposed_products(step):
        def body(part, carry):
            for i in range(half // BEHIND_PARTS):
                j = part * (half // BEHIND_PARTS) + i
                if step == 0:
                    for c in range(CHAINS):
                        load(c * half + j).wait()
                for k in range(0, kt, 2):
                    for c in range(CHAINS):
                        add_pair(step, c, j, k)
            return carry

        lax.fori_loop(0, BEHIND_PARTS, body, 0)

    def add_pair(step, c, j, k):
        r = c * half + j
        pair = jnp.concatenate([tiles[r, k], tiles[r, k + 1]], axis=1)
        both = jnp.dot(win[step][:, block(own + r)], pair, preferred_element_type=F32)
        for i in range(2):
            slot = tab_s[SLOT_ROW + r, k + i]
            weight = jnp.where(slot == own + r, 0.5, 1.0).astype(F32)
            part = both[:, i * width : (i + 1) * width] * weight
            before = tab_s[r, k + i]
            sums[c][j * kt + k + i] = part + sums[c][before]

    def slot_sum(s):
        return sum(sums[c][tab_s[LAST_ROW + 8 * c, s]] for c in range(CHAINS))

    def stage_products(step):
        for i in range(2):
            for r in range(rows):
                staged[step, i, r] = slot_sum((2 * i + 1) * rows + r)

    def send_products(step):
        for i in range(2):
            share_copy(step, i).start()
        if step == 0:
            pl.when(chip < LINE - 2)(lambda: send_vectors(0))
        for i in range(2):
            if i == 0:
                pl.when(core == 1)(lambda: await_share(step, 0))
            else:
                await_share(step, 1)
                pl.when(gathers)(relay_copy(step).wait_recv)
                power = relayed[step, rows].astype(jnp.int32).astype(F32)
                unit = jnp.exp2(power) * (1.0 / TOP)
            most = jnp.zeros((nv, width), F32)
            for r in range(rows):
                v = slot_sum(2 * i * rows + r) + shared[step, i, r]
                if i == 1:
                    v = v + relayed[step, r].astype(jnp.int32).astype(F32) * unit
                total[r] = v
                most = jnp.maximum(most, jnp.abs(v))
            peak = jnp.maximum(jnp.max(most, axis=1, keepdims=True), 1e-30)
            power = jnp.broadcast_to(jnp.ceil(jnp.log2(peak)), (nv, width))
            scale = jnp.exp2(-power) * TOP
            for r in range(rows):
                coded[step, i, r] = (
                    jnp.round(total[r] * scale).astype(jnp.int32).astype(jnp.int16)
                )
            coded[step, i, rows] = power.astype(jnp.int32).astype(jnp.int16)
            pl.when(goes[i])(product_copy(step, i).start)
            if i == 0:
                pl.when(relays)(relay_copy(step).start)

    def turn():
        def body(r, carry):
            for k in range(kt):
                turned[r, k * width : (k + 1) * width, :] = tiles[r, k].T
            return carry

        lax.fori_loop(0, rows, body, 0)

    def forward(step):
        for s in range(own + rows):
            blocks[s] = win[step][:, block(s)]

        def body(part, carry):
            for i in range(rows // FORWARD_PARTS):
                r = part * (rows // FORWARD_PARTS) + i
                picked = []
                for k in range(kt):
                    slot = tab_s[SLOT_ROW + r, k]
                    weight = jnp.full((nv, width), jnp.where(slot == own + r, 0.5, 1.0), F32)
                    picked.append(blocks[slot] * weight.astype(jnp.bfloat16))
                x = jnp.concatenate(picked, axis=1)
                ahead[r] = jnp.dot(x, turned[r], preferred_element_type=F32)
            return carry

        lax.fori_loop(0, FORWARD_PARTS, body, 0)

    for copy in smalls[3:]:
        copy.wait()
    center = center_s[0]
    inv = 1.0 / jnp.full((nv, width), half_s[0], F32)

    shift[...] = jnp.broadcast_to((center * inv)[:1, :1], shift.shape)

    greeted = 1 + jnp.minimum(me // 2, 2) + jnp.minimum((n - 1 - me) // 2, 2)
    greeted = greeted - jnp.where(relays, 1, 0)
    def enter():
        pl.semaphore_wait(barrier, greeted)
        send_vectors(0)

    for step in range(2):
        if step == 0:
            tab_copy.wait()
            smalls[2].wait()

            @pl.when(chip >= LINE - 2)
            def _():
                enter()
        else:
            send_vectors(step)
        transposed_products(step)
        stage_products(step)
        if step == 0:

            @pl.when(chip < LINE - 2)
            def _():
                pl.semaphore_wait(barrier, greeted)
        send_products(step)
        if step == 0:
            turn()
        for g, copy, wanted in vector_hands(step):
            await_vectors(step, g)
            pl.when(wanted)(copy.start)
        for g in (1, 3):
            await_vectors(step, g)
        forward(step)
        pl.when(core == 0)(lambda: await_share(step, 2))
        scales = []
        for i in range(2):
            pl.when(comes[i])(product_copy(step, i).wait_recv)
        for i in range(2):
            power = landed[step, i, rows].astype(jnp.int32).astype(F32)
            scales.append(jnp.exp2(power) * (1.0 / TOP))
        for r in range(rows):
            cut = slice(r * width, (r + 1) * width)
            v = ahead[r] + slot_sum(own + r) + shared[step, 2, r]
            for i in range(2):
                v = v + landed[step, i, r].astype(jnp.int32).astype(F32) * scales[i]
            if step == 0:
                out1[:, cut] = v * inv
                first[r] = v * inv - win0[:, block(own + r)].astype(F32) * (center * inv)
                win1[:, block(own + r)] = first[r].astype(jnp.bfloat16)
            else:
                out2[:, cut] = 2.0 * (v - center * first[r]) * inv

    for step in range(2):
        for wanted, copy in vector_sends(step):
            pl.when(wanted)(copy.wait_send)
        for g, copy, wanted in vector_hands(step):
            pl.when(wanted)(copy.wait_send)
        for i in range(2):
            share_copy(step, i).wait_send()
            pl.when(goes[i])(product_copy(step, i).wait_send)
        pl.when(relays)(relay_copy(step).wait_send)


def per_device(n, matrix_tiles, columns, vectors, center, halfwidth):
    rows, kt, width, _ = matrix_tiles.shape
    nv = vectors.shape[0]
    hbm = pl.BlockSpec(memory_space=pltpu.HBM)
    vmem = pl.BlockSpec(memory_space=pltpu.VMEM)
    out = jax.ShapeDtypeStruct(vectors.shape, F32)
    chain = rows // CHAINS * kt
    pinned = [
        pltpu.with_memory_space_constraint(a, pltpu.HBM)
        for a in (matrix_tiles, columns, vectors)
    ]
    one, two, shift = pl.pallas_call(
        functools.partial(kernel, n),
        out_shape=(out, out, jax.ShapeDtypeStruct((1, vectors.shape[1]), F32)),
        in_specs=[hbm] * 3 + [pl.BlockSpec(memory_space=pl.ANY)] * 2,
        out_specs=(vmem, vmem, vmem),
        scratch_shapes=[
            pltpu.VMEM(columns.shape, jnp.int32),
            pltpu.SMEM(columns.shape, jnp.int32),
            pltpu.SMEM((1,), F32),
            pltpu.SMEM((1,), F32),
            pltpu.VMEM(matrix_tiles.shape, jnp.bfloat16),
            pltpu.VMEM((rows, kt * width, width), jnp.bfloat16),
            pltpu.VMEM((nv, (SPAN + 1) * vectors.shape[1]), jnp.bfloat16),
            pltpu.VMEM((nv, (SPAN + 1) * vectors.shape[1]), jnp.bfloat16),
            pltpu.VMEM(((SPAN + 1) * rows, nv, width), jnp.bfloat16),
            [pltpu.VMEM((chain + 1, nv, width), F32)] * CHAINS,
            pltpu.VMEM((rows, nv, width), F32),
            pltpu.VMEM((rows, nv, width), F32),
            pltpu.VMEM((rows, nv, width), F32),
            pltpu.VMEM((2, 2, rows, nv, width), F32),
            pltpu.VMEM((2, 3, rows, nv, width), F32),
            pltpu.VMEM((2, 2, rows + 1, nv, width), jnp.int16),
            pltpu.VMEM((2, 2, rows + 1, nv, width), jnp.int16),
            pltpu.VMEM((2, rows + 1, nv, width), jnp.int16),
            pltpu.VMEM((SLOT_ROW + rows, 128), jnp.int32),
            pltpu.SMEM((SLOT_ROW + rows, 128), jnp.int32),
            pltpu.SemaphoreType.DMA((rows,)),
            pltpu.SemaphoreType.DMA((5,)),
            pltpu.SemaphoreType.DMA,
            pltpu.SemaphoreType.DMA((2, SPAN + 1)),
            pltpu.SemaphoreType.DMA((2, SPAN)),
            pltpu.SemaphoreType.DMA((2, 2)),
            pltpu.SemaphoreType.DMA((2, 3)),
            pltpu.SemaphoreType.DMA((2, 2)),
            pltpu.SemaphoreType.DMA((2, 2)),
            pltpu.SemaphoreType.DMA((2,)),
        ],
        compiler_params=pltpu.CompilerParams(
            collective_id=0, has_side_effects=True, vmem_limit_bytes=32 << 20
        ),
    )(*pinned, center, halfwidth)
    initial = vectors.astype(F32)
    return one - initial * shift, two - initial


def solution(mesh):
    placed = (P("tri", None, None, None), P("tri", None), P(None, "tri"), P(), P())
    return jax.shard_map(
        functools.partial(per_device, mesh.shape["tri"]),
        mesh=mesh,
        in_specs=placed,
        out_specs=(P(None, "tri"), P(None, "tri")),
        check_vma=False,
    )
```
